32 devices in a mesh: fsdp: 16 (over z, x, core), tensor: 2 (over y).
Axes of the slice: x: 2, y: 2, z: 4, core: 2. Of those that a mesh axis runs over, the one named last changes fastest.
Arguments:
- hidden_in: bfloat16 [8192, 5120], P('fsdp', 'tensor'), may hold values from -80 to 80
- norm_gain: bfloat16 [5120], replicated, may hold values from 0.099609375 to 1.8984375
- query_weight: bfloat16 [5120, 5120], P(('fsdp', 'tensor')), may hold values from -0.078125 to 0.078125
- key_weight: bfloat16 [5120, 1024], P(('fsdp', 'tensor')), may hold values from -0.078125 to 0.078125
- value_weight: bfloat16 [5120, 1024], P(('fsdp', 'tensor')), may hold values from -0.078125 to 0.078125
- out_weight: bfloat16 [5120, 5120], P(('fsdp', 'tensor')), may hold values from -0.078125 to 0.078125
- query_bias: bfloat16 [5120], P('tensor'), may hold values from -10.5 to 10.5
- key_bias: bfloat16 [1024], P('tensor'), may hold values from -5.5 to 5.5
- value_bias: bfloat16 [1024], P('tensor'), may hold values from -3 to 3
- span_start: int32 [32], P('fsdp'), may hold values from 0 to 3839
- span_length: int32 [32], P('fsdp'), may hold values from 64 to 256, as said below
Outputs:
- attention_out: bfloat16 [8192, 5120], P('fsdp', 'tensor')
- key_cache: bfloat16 [8192, 1024], P('fsdp', 'tensor')
- value_cache: bfloat16 [8192, 1024], P('fsdp', 'tensor')
The draws below stay inside these ranges and needn't reach their ends.
Inputs may be any that keep to these rules, and one draw needn't show every extreme that they name: `span_length`: the spans of the first rollout group are all full.
All inputs are finite; a program needn't handle non-finite values.
Results may differ from the reference program's by a relative error of at most 0.0065.
The reference program's roundings to bfloat16 on the way count: a program that leaves them out, or rounds other values in their place, can miss the bound.
Values may be sent and summed in bfloat16 or wider, within the bound.
A program may use at most 192 MiB of HBM per device.

```python
import jax
import jax.numpy as jnp
from jax import lax

D = 5120
HEADS = 40
KV_HEADS = 8
HEAD = 128
SPAN = 256
SEQS = 2
MAXPOS = 4096
SPANS = 32
TOKENS = 8192


def draw_hidden_in(key, part):
    base_key = jax.random.fold_in(key, 101)
    row_key = jax.random.fold_in(key, 102)
    column_key = jax.random.fold_in(key, 103)
    base = jnp.clip(jax.random.normal(base_key, (TOKENS, D), jnp.float32), -4.0, 4.0)
    row_scale = 0.3 * jnp.exp(jax.random.uniform(row_key, (TOKENS, 1), jnp.float32) * jnp.log(10.0))
    ramp = jnp.exp(jnp.log(10.0) * (jnp.arange(D, dtype=jnp.float32) / D - 0.5))
    jitter = jnp.exp(jax.random.uniform(column_key, (D,), jnp.float32) * jnp.log(2.0))
    return (base * row_scale * (ramp * jitter)[None, :]).astype(jnp.bfloat16)


def bias_pair(key):
    query_part = 0.5 * jnp.clip(jax.random.normal(jax.random.fold_in(key, 205), (HEADS, HEAD), jnp.float32), -3.0, 3.0)
    key_part = 0.5 * jnp.clip(jax.random.normal(jax.random.fold_in(key, 206), (KV_HEADS, HEAD), jnp.float32), -3.0, 3.0)
    return (query_part.reshape(HEADS * HEAD), key_part.reshape(KV_HEADS * HEAD))


def draw_query_bias(key, part):
    return bias_pair(key)[0].astype(jnp.bfloat16)


def draw_key_bias(key, part):
    return bias_pair(key)[1].astype(jnp.bfloat16)


def draw_span_length(key, part):
    lengths = jax.random.randint(jax.random.fold_in(key, 301), (SPANS,), SPAN // 4, SPAN + 1, dtype=jnp.int32)
    return lengths.at[:SEQS].set(SPAN)


def set_ends(values, own_key, least, top_value):
    longest = values.shape.index(max(values.shape))
    spots = []
    for shift in (0, 1):
        where = [jax.random.randint(jax.random.fold_in(own_key, axis), (), 0, length) for axis, length in enumerate(values.shape)]
        where[longest] = (where[longest] + shift) % values.shape[longest]
        spots.append(tuple(where))
    return values.at[spots[0]].set(least).at[spots[1]].set(top_value)


def steps_of(own_key, dims, cuts, least, largest):
    loudness = 1.0
    for position, shards_of in cuts:
        heights = jax.random.uniform(jax.random.fold_in(jax.random.fold_in(own_key, 6), position), (shards_of,), jnp.float32, least / len(cuts), largest / len(cuts))
        loudness = loudness * jnp.repeat(jnp.exp(heights), dims[position] // shards_of).reshape((-1,) + (1,) * (len(dims) - 1 - position))
    return loudness


def bell_draw(rng, dims, width, limit, split=(), held_as=jnp.bfloat16):
    gain = steps_of(rng, dims, split, -0.22, 0.18) if split else 1.0
    values = jax.random.normal(rng, dims, jnp.float32) * width * gain
    return jnp.minimum(jnp.maximum(values, -limit), limit).astype(held_as)


def setup_inputs(seed: int = 0) -> dict:
    arg_keys = jax.random.split(jax.random.key(seed), 12)
    hidden_in = draw_hidden_in(jax.random.fold_in(arg_keys[11], 71), 0)
    norm_gain = jnp.clip(1.0 + 0.18 * jax.random.normal(arg_keys[1], (D,), jnp.float32), 0.099609375, 1.8984375).astype(jnp.bfloat16)
    query_weight = bell_draw(arg_keys[2], (D, HEADS * HEAD), D ** -0.5, 0.078125, ((0, 32),))
    key_weight = bell_draw(arg_keys[3], (D, KV_HEADS * HEAD), D ** -0.5, 0.078125, ((0, 32),))
    value_weight = bell_draw(arg_keys[4], (D, KV_HEADS * HEAD), D ** -0.5, 0.078125, ((0, 32),))
    out_weight = bell_draw(arg_keys[5], (HEADS * HEAD, D), (HEADS * HEAD) ** -0.5, 0.078125, ((0, 32),))
    query_bias = draw_query_bias(jax.random.fold_in(arg_keys[11], 71), 0)
    key_bias = draw_key_bias(jax.random.fold_in(arg_keys[11], 71), 0)
    value_bias = bell_draw(arg_keys[8], (KV_HEADS * HEAD,), 0.5, 3.0, ((0, 2),))
    span_start = set_ends(jax.random.randint(arg_keys[9], (SPANS,), 0, MAXPOS - SPAN), jax.random.fold_in(arg_keys[9], 1), 0, (MAXPOS - SPAN) - 1).astype(jnp.int32)
    span_length = draw_span_length(jax.random.fold_in(arg_keys[11], 71), 0)
    return {"hidden_in": hidden_in, "norm_gain": norm_gain, "query_weight": query_weight, "key_weight": key_weight, "value_weight": value_weight, "out_weight": out_weight, "query_bias": query_bias, "key_bias": key_bias, "value_bias": value_bias, "span_start": span_start, "span_length": span_length}


rope_base = 1000000.0
epsilon = 1e-06

def rotate(entries, cosine, sine):
    half = entries.shape[-1] // 2
    first = entries[..., :half]
    second = entries[..., half:]
    return jnp.concatenate([first * cosine - second * sine, second * cosine + first * sine], axis=-1)

def angles(span_start, span_size):
    positions = span_start[:, None] + jnp.arange(span_size, dtype=jnp.int32)[None, :]
    inverse = 1.0 / rope_base ** (jnp.arange(0, HEAD, 2, dtype=jnp.float32) / HEAD)
    phase = positions.reshape(-1).astype(jnp.float32)[:, None] * inverse[None, :]
    return (jnp.cos(phase)[:, None, :], jnp.sin(phase)[:, None, :])

def reference(hidden_in, norm_gain, query_weight, key_weight, value_weight, out_weight, query_bias, key_bias, value_bias, span_start, span_length):
    source = hidden_in.astype(jnp.float32)
    inverse_rms = lax.rsqrt(lax.optimization_barrier(jnp.mean(source * source, axis=-1, keepdims=True)) + epsilon)
    normed = (source * inverse_rms * norm_gain.astype(jnp.float32)).astype(jnp.bfloat16)
    query = jnp.dot(normed, query_weight, preferred_element_type=jnp.float32) + query_bias.astype(jnp.float32)
    keys = jnp.dot(normed, key_weight, preferred_element_type=jnp.float32) + key_bias.astype(jnp.float32)
    values = jnp.dot(normed, value_weight, preferred_element_type=jnp.float32) + value_bias.astype(jnp.float32)
    cosine, sine = angles(span_start, SPAN)
    query = rotate(query.reshape(TOKENS, HEADS, HEAD), cosine, sine).astype(jnp.bfloat16)
    keys = rotate(keys.reshape(TOKENS, KV_HEADS, HEAD), cosine, sine)
    live = (jnp.arange(SPAN, dtype=jnp.int32)[None, :] < span_length[:, None]).reshape(TOKENS, 1, 1)
    key_cache = jnp.where(live, keys, 0.0).astype(jnp.bfloat16)
    value_cache = jnp.where(live, values.reshape(TOKENS, KV_HEADS, HEAD), 0.0).astype(jnp.bfloat16)
    groups = HEADS // KV_HEADS

    def attend(item):
        query_block, key_block, value_block, length = item
        query_wide = query_block.astype(jnp.float32).reshape(SPAN, KV_HEADS, groups, HEAD)
        scores = jnp.einsum('qkgd,tkd->kgqt', query_wide, key_block.astype(jnp.float32)) * HEAD ** (-0.5)
        rows = jnp.arange(SPAN, dtype=jnp.int32)[:, None]
        columns = jnp.arange(SPAN, dtype=jnp.int32)[None, :]
        allowed = (columns <= rows) & (columns < length)
        scores = jnp.where(allowed, scores, -1e+30)
        highest = lax.optimization_barrier(jnp.max(scores, axis=-1, keepdims=True))
        raised = jnp.exp(scores - highest)
        probs = (raised / lax.optimization_barrier(jnp.sum(raised, axis=-1, keepdims=True))).astype(jnp.bfloat16)
        mixed = jnp.einsum('kgqt,tkd->qkgd', probs.astype(jnp.float32), value_block.astype(jnp.float32))
        return mixed.reshape(SPAN, HEADS * HEAD).astype(jnp.bfloat16)
    attended = lax.map(attend, (query.reshape(SPANS, SPAN, HEADS, HEAD), key_cache.reshape(SPANS, SPAN, KV_HEADS, HEAD), value_cache.reshape(SPANS, SPAN, KV_HEADS, HEAD), span_length))
    attended = attended.reshape(TOKENS, HEADS * HEAD)
    attention_out = jnp.dot(attended, out_weight, preferred_element_type=jnp.float32).astype(jnp.bfloat16)
    return (attention_out, key_cache.reshape(TOKENS, KV_HEADS * HEAD), value_cache.reshape(TOKENS, KV_HEADS * HEAD))
```

```python
import jax
import jax.numpy as jnp
from jax import lax
from jax.sharding import PartitionSpec as P

HEADS = 40
KV_HEADS = 8
HEAD = 128
GROUPS = HEADS // KV_HEADS
AXES = ("fsdp", "tensor")

rope_base = 1000000.0
epsilon = 1e-06


def rotate(entries, cosine, sine):
    half = entries.shape[-1] // 2
    first = entries[..., :half]
    second = entries[..., half:]
    return jnp.concatenate(
        [first * cosine - second * sine, second * cosine + first * sine], axis=-1
    )


def angles(span_start, span_size):
    positions = span_start[:, None] + jnp.arange(span_size, dtype=jnp.int32)[None, :]
    inverse = 1.0 / rope_base ** (jnp.arange(0, HEAD, 2, dtype=jnp.float32) / HEAD)
    phase = positions.reshape(-1).astype(jnp.float32)[:, None] * inverse[None, :]
    return (jnp.cos(phase)[:, None, :], jnp.sin(phase)[:, None, :])


def local(
    hidden_in,
    norm_gain,
    query_weight,
    key_weight,
    value_weight,
    out_weight,
    query_bias,
    key_bias,
    value_bias,
    span_start,
    span_length,
):
    slices = lax.axis_size("tensor")
    members = lax.axis_size("fsdp")
    devices = slices * members
    inner = KV_HEADS // slices
    outer = devices // KV_HEADS
    line = lax.axis_index("fsdp") // inner
    i = lax.axis_index("fsdp") % inner
    t = lax.axis_index("tensor")
    token_rows, features = hidden_in.shape
    local_spans = span_start.shape[0]
    span_size = token_rows // local_spans
    learner_rows = query_weight.shape[0]
    qc = GROUPS * HEAD
    oc = out_weight.shape[1] // KV_HEADS

    def xor(x, k):
        return lax.ppermute(x, AXES, [(d, d ^ k) for d in range(devices)])

    def shift(x, step):
        pairs = [
            (d, d + step * KV_HEADS)
            for d in range(devices)
            if 0 <= d + step * KV_HEADS < devices
        ]
        return lax.ppermute(x, AXES, pairs)

    def gather_group(own):
        half = own.shape[0] // 2
        one = xor(own, 1)
        four = xor(own, 4)
        five = jnp.concatenate([xor(four[:half], 1), xor(one[half:], 4)], axis=0)
        got = {0: own, 1: one, 4: four, 5: five}
        for k in (0, 1, 4, 5):
            got[k ^ 2] = xor(got[k], 2)
        return [got[k] for k in range(KV_HEADS)]

    def blocks(weight):
        cols = weight.shape[1] // KV_HEADS
        cut = weight.reshape(learner_rows, slices, inner, cols)
        return jnp.transpose(cut, (2, 1, 0, 3)).reshape(KV_HEADS, learner_rows, cols)

    def exchange(stacked):
        groups = [[g * KV_HEADS + j for j in range(KV_HEADS)] for g in range(outer)]
        arrived = lax.all_to_all(
            stacked, AXES, split_axis=0, concat_axis=0, axis_index_groups=groups, tiled=True
        )
        return arrived.reshape(KV_HEADS * learner_rows, stacked.shape[2])

    def gather_line(slab):
        below, above = [], []
        up = down = slab
        for _ in range(outer - 1):
            up = shift(up, 1)
            down = shift(down, -1)
            below.append(up)
            above.append(down)
        every = jnp.stack(below[::-1] + [slab] + above)
        whole = lax.dynamic_slice_in_dim(every, outer - 1 - line, outer, axis=0)
        return whole.reshape(outer * slab.shape[0], slab.shape[1])

    def unswap(parts):
        parts = list(parts)
        bit = 1
        while bit < inner:
            flip = (i & bit) != 0
            parts = [jnp.where(flip, parts[p ^ bit], parts[p]) for p in range(inner)]
            bit *= 2
        return parts

    joined = jnp.concatenate(
        [blocks(query_weight), blocks(key_weight), blocks(value_weight)], axis=2
    )
    weight = gather_line(exchange(joined))
    out_whole = gather_line(exchange(blocks(out_weight)))

    source = hidden_in.astype(jnp.float32)
    squares = jnp.sum(source * source, axis=-1, keepdims=True)
    bit = 1
    while bit < slices:
        squares = squares + xor(squares, bit)
        bit *= 2
    inverse_rms = lax.rsqrt(squares / (features * slices) + epsilon)
    gain = lax.dynamic_slice_in_dim(norm_gain, t * features, features).astype(jnp.float32)
    normed = (source * inverse_rms * gain).astype(jnp.bfloat16)
    tokens = gather_group(normed)
    spans = lax.all_gather(jnp.stack([span_start, span_length]), "fsdp", axis=1, tiled=True)

    bias = jnp.concatenate(
        [
            lax.dynamic_slice_in_dim(query_bias, i * qc, qc),
            lax.dynamic_slice_in_dim(key_bias, i * HEAD, HEAD),
            lax.dynamic_slice_in_dim(value_bias, i * HEAD, HEAD),
        ]
    ).astype(jnp.float32)
    rows = jnp.arange(span_size, dtype=jnp.int32)[:, None]
    columns = jnp.arange(span_size, dtype=jnp.int32)[None, :]
    halves = [
        lax.dynamic_slice_in_dim(weight, (t ^ kt) * features, features) for kt in range(slices)
    ]
    mixes, key_parts, value_parts = [], [], []
    for ki in range(inner):
        projected = bias[None, :]
        for kt in range(slices):
            projected = projected + jnp.dot(
                tokens[ki * slices + kt], halves[kt], preferred_element_type=jnp.float32
            )
        own = lax.dynamic_slice_in_dim(
            spans, (line * inner + (i ^ ki)) * local_spans, local_spans, axis=1
        )
        start, length = own[0], own[1]
        cosine, sine = angles(start, span_size)
        query = rotate(
            projected[:, :qc].reshape(token_rows, GROUPS, HEAD), cosine, sine
        ).astype(jnp.bfloat16)
        keys = rotate(projected[:, None, qc : qc + HEAD], cosine, sine)[:, 0]
        live = (columns < length[:, None]).reshape(token_rows, 1)
        key_cache = jnp.where(live, keys, 0.0).astype(jnp.bfloat16)
        value_cache = jnp.where(live, projected[:, qc + HEAD :], 0.0).astype(jnp.bfloat16)
        query_blocks = query.reshape(local_spans, span_size, GROUPS, HEAD)
        key_blocks = key_cache.reshape(local_spans, span_size, HEAD)
        value_blocks = value_cache.reshape(local_spans, span_size, HEAD)
        scores = jnp.einsum(
            "sqgd,std->sgqt", query_blocks, key_blocks, preferred_element_type=jnp.float32
        ) * HEAD ** (-0.5)
        allowed = (columns <= rows)[None] & (columns[None] < length[:, None, None])
        scores = jnp.where(allowed[:, None], scores, -1e30)
        highest = jnp.max(scores, axis=-1, keepdims=True)
        raised = jnp.exp(scores - highest)
        probs = (raised / jnp.sum(raised, axis=-1, keepdims=True)).astype(jnp.bfloat16)
        mixed = jnp.einsum(
            "sgqt,std->sqgd", probs, value_blocks, preferred_element_type=jnp.float32
        )
        mixes.append(mixed.reshape(token_rows, qc).astype(jnp.bfloat16))
        key_parts.append(key_cache if ki == 0 else xor(key_cache, ki * slices))
        value_parts.append(value_cache if ki == 0 else xor(value_cache, ki * slices))

    mixes = unswap(mixes)
    attended = gather_group(jnp.concatenate(mixes, axis=0))
    combined = 0.0
    for k in range(KV_HEADS):
        head = (t ^ (k % slices)) * inner + (i ^ (k // slices))
        combined = combined + jnp.dot(
            attended[k],
            lax.dynamic_slice_in_dim(out_whole, head * qc, qc),
            preferred_element_type=jnp.float32,
        )
    result = combined.astype(jnp.bfloat16).reshape(inner, token_rows, oc)
    result = unswap([result[p] for p in range(inner)])
    out_parts = [result[0]] + [xor(result[ki], ki * slices) for ki in range(1, inner)]
    return tuple(
        jnp.concatenate(unswap(parts), axis=1)
        for parts in (out_parts, key_parts, value_parts)
    )


def solution(mesh):
    placed = (
        P("fsdp", "tensor"),
        P(),
        P(("fsdp", "tensor"), None),
        P(("fsdp", "tensor"), None),
        P(("fsdp", "tensor"), None),
        P(("fsdp", "tensor"), None),
        P("tensor"),
        P("tensor"),
        P("tensor"),
        P("fsdp"),
        P("fsdp"),
    )
    return jax.shard_map(
        local,
        mesh=mesh,
        in_specs=placed,
        out_specs=(P("fsdp", "tensor"), P("fsdp", "tensor"), P("fsdp", "tensor")),
        check_vma=False,
    )
```

```python
import functools

import jax
import jax.numpy as jnp
from jax import lax
from jax.experimental import pallas as pl
from jax.experimental.pallas import tpu as pltpu
from jax.sharding import PartitionSpec as P

HEADS = 40
KV_HEADS = 8
HEAD = 128
GROUPS = HEADS // KV_HEADS
AXES = ("fsdp", "tensor")

rope_base = 1000000.0
epsilon = 1e-06


def rotate(entries, cosine, sine):
    half = entries.shape[-1] // 2
    first = entries[..., :half]
    second = entries[..., half:]
    return jnp.concatenate(
        [first * cosine - second * sine, second * cosine + first * sine], axis=-1
    )


def angles(span_start, span_size):
    positions = span_start[:, None] + jnp.arange(span_size, dtype=jnp.int32)[None, :]
    inverse = 1.0 / rope_base ** (jnp.arange(0, HEAD, 2, dtype=jnp.float32) / HEAD)
    phase = positions.reshape(-1).astype(jnp.float32)[:, None] * inverse[None, :]
    return (jnp.cos(phase)[:, None, :], jnp.sin(phase)[:, None, :])


MESH = pl.DeviceIdType.MESH
G = KV_HEADS
QC = GROUPS * HEAD


def flip(m, bit):
    return m + bit - 2 * bit * (lax.div(m, bit) % 2)


def body(
    members, slices, spans, span_size,
    normed, joined, outs, bias, cosine, sine, length,
    out, key_out, value_out, gathered,
    wq, wo, tokens, own, keys, values, result, buffer,
    a_send, a_recv, a_own, b_send, b_recv, b_own,
    zq_send, zq_recv, zo_send, zo_recv,
    t_send, t_recv, t_own, g_send, g_recv, g_own,
    load, r_send, r_recv, k_send, k_recv, v_send, v_recv,
):
    inner = G // slices
    line_size = members // inner
    f = lax.axis_index("fsdp")
    t = lax.axis_index("tensor")
    o = lax.div(f, inner)
    i = f % inner
    me = i * slices + t
    rows = joined.shape[1]
    mx, my, mc = flip(me, 4), flip(me, 1), flip(me, 2)
    md = flip(mx, 1)

    def member(m):
        return (o * inner + lax.div(m, slices), m % slices)

    def remote(src, dst, ss, rs, where):
        return pltpu.make_async_remote_copy(
            src_ref=src, dst_ref=dst, send_sem=ss, recv_sem=rs, device_id=where, device_id_type=MESH
        )

    barrier = pltpu.get_barrier_semaphore()
    for d in range(1, G):
        pl.semaphore_signal(
            barrier, inc=1, device_id=member((me + d) % G), device_id_type=MESH
        )

    @pl.when(o > 0)
    def _():
        pl.semaphore_signal(barrier, inc=1, device_id=(f - inner, t), device_id_type=MESH)

    @pl.when(o < line_size - 1)
    def _():
        pl.semaphore_signal(barrier, inc=1, device_id=(f + inner, t), device_id_type=MESH)

    ends = (o == 0).astype(jnp.int32) + (o == line_size - 1).astype(jnp.int32)
    pl.semaphore_wait(barrier, G + 1 - ends)

    def place(buf, origin, m, count):
        return buf.at[pl.ds(pl.multiple_of((origin * G + m) * rows, rows), count * rows), :]

    def trade(src, buf, ss, rs, d):
        to = (me + d) % G
        return remote(src.at[to], place(buf, o, me, 1), ss.at[d], rs.at[d], member(to))

    def trade_own(src, buf, sem):
        return pltpu.make_async_copy(src.at[me], place(buf, o, me, 1), sem)

    def trade_start(src, buf, ss, rs, sem):
        trade_own(src, buf, sem).start()
        for d in range(1, G):
            trade(src, buf, ss, rs, d).start()

    def trade_wait(src, buf, ss, rs, sem, m):
        @pl.when(m == me)
        def _():
            trade_own(src, buf, sem).wait()

        @pl.when(m != me)
        def _():
            d = (me - m + G) % G
            here = place(buf, o, m, 1)
            remote(here, here, ss.at[d], rs.at[d], member(m)).wait_recv()

    def hop(buf, ss, rs, origin, c, way):
        here = place(buf, origin, 2 * c, 2)
        way_f = f + inner if way == 0 else f - inner
        return remote(here, here, ss.at[way, origin, c], rs.at[origin, c], (way_f, t))

    def forward(buf, ss, rs, s, c):
        below, above = o - s, o + s
        if s > 0:
            @pl.when(below >= 0)
            def _():
                hop(buf, ss, rs, below, c, 0).wait_recv()

            @pl.when(above < line_size)
            def _():
                hop(buf, ss, rs, above, c, 0).wait_recv()

        @pl.when(jnp.logical_and(below >= 0, o < line_size - 1))
        def _():
            hop(buf, ss, rs, below, c, 0).start()

        @pl.when(jnp.logical_and(above < line_size, o > 0))
        def _():
            hop(buf, ss, rs, above, c, 1).start()

    def hops_sent(buf, ss, rs):
        for s in range(line_size):
            for c in range(G // 2):
                below, above = o - s, o + s

                @pl.when(jnp.logical_and(below >= 0, o < line_size - 1))
                def _():
                    hop(buf, ss, rs, below, c, 0).wait_send()

                @pl.when(jnp.logical_and(above < line_size, o > 0))
                def _():
                    hop(buf, ss, rs, above, c, 1).wait_send()

    def piece(buf, m, n):
        return buf.at[m, pl.ds(pl.multiple_of(n * span_size, span_size), span_size), :]

    def mine(src, n):
        return src.at[pl.ds(pl.multiple_of(n * span_size, span_size), span_size), :]

    def send_own(src, buf, ss, rs, sem, n):
        for kind, to in ((0, mx), (1, my), (2, mc)):
            remote(
                mine(src, n), piece(buf, me, n), ss.at[kind, n], rs.at[kind, n], member(to)
            ).start()
        pltpu.make_async_copy(mine(src, n), piece(buf, me, n), sem.at[n]).start()

    def arrived(buf, ss, rs, kind, slot, n):
        here = piece(buf, slot, n)
        remote(here, here, ss.at[kind, n], rs.at[kind, n], member(mx)).wait_recv()

    def pass_on(buf, ss, rs, kind, slot, to, n):
        here = piece(buf, slot, n)
        remote(here, here, ss.at[kind, n], rs.at[kind, n], member(to)).start()

    def relay(buf, ss, rs, n, total):
        arrived(buf, ss, rs, 0, mx, n)
        arrived(buf, ss, rs, 1, my, n)

        @pl.when(n < total // 2)
        def _():
            pass_on(buf, ss, rs, 3, mx, my, n)

        @pl.when(n >= total // 2)
        def _():
            pass_on(buf, ss, rs, 3, my, mx, n)

        pass_on(buf, ss, rs, 4, mx, mc, n)
        pass_on(buf, ss, rs, 5, my, mc, n)

    def relay_far(buf, ss, rs, n):
        arrived(buf, ss, rs, 3, md, n)
        pass_on(buf, ss, rs, 6, md, mc, n)

    def settle(src, buf, ss, rs, sem, n):
        pltpu.make_async_copy(mine(src, n), piece(buf, me, n), sem.at[n]).wait()
        for kind, slot in ((2, mc), (4, flip(mx, 2)), (5, flip(my, 2)), (6, flip(md, 2))):
            arrived(buf, ss, rs, kind, slot, n)

    def sent(buf, ss, rs, n):
        for kind in range(7):
            here = piece(buf, me, n)
            remote(here, here, ss.at[kind, n], rs.at[kind, n], member(mx)).wait_send()

    trade_start(joined, wq, a_send, a_recv, a_own)
    for n in range(spans):
        send_own(normed, tokens, t_send, t_recv, t_own, n)
    for c in range(G // 2):
        for m in (2 * c, 2 * c + 1):
            trade_wait(joined, wq, a_send, a_recv, a_own, m)
        forward(wq, zq_send, zq_recv, 0, c)
    for n in range(spans):
        relay(tokens, t_send, t_recv, n, spans)
    for c in range(G // 2):
        forward(wq, zq_send, zq_recv, 1, c)
    trade_start(outs, wo, b_send, b_recv, b_own)
    for n in range(spans):
        relay_far(tokens, t_send, t_recv, n)
    for s in range(2, line_size):
        if s == line_size - 1:
            for c in range(G // 2):
                for m in (2 * c, 2 * c + 1):
                    trade_wait(outs, wo, b_send, b_recv, b_own, m)
                forward(wo, zo_send, zo_recv, 0, c)
        for c in range(G // 2):
            forward(wq, zq_send, zq_recv, s, c)
    for n in range(spans):
        settle(normed, tokens, t_send, t_recv, t_own, n)

    pieces = inner * spans
    features = tokens.shape[2]
    scale = HEAD ** (-0.5)

    def chunk_copy(stage, target, ss, rs, p):
        src = stage.at[pl.ds(pl.multiple_of(p * spans * span_size, span_size), spans * span_size), :]
        dst = target.at[:, pl.ds(pl.multiple_of(i * HEAD, HEAD), HEAD)]
        return (
            pltpu.make_async_copy(src, dst, ss.at[p]),
            remote(src, dst, ss.at[p], rs.at[i], (o * inner + p, t)),
        )

    def chunk_arrived(stage, target, ss, rs, p):
        src = stage.at[pl.ds(0, spans * span_size), :]
        dst = target.at[:, pl.ds(pl.multiple_of(p * HEAD, HEAD), HEAD)]
        remote(src, dst, ss.at[p], rs.at[p], (o * inner + p, t)).wait_recv()

    def one_span(n, carry):
        p = lax.div(n, spans)
        part = n % spans
        here = pl.ds(pl.multiple_of(n * span_size, span_size), span_size)
        projected = bias[...]
        for half in range(slices):
            projected = projected + jnp.dot(
                tokens[p * slices + half, pl.ds(pl.multiple_of(part * span_size, span_size), span_size), :],
                wq[pl.ds(half * features, features), :],
                preferred_element_type=jnp.float32,
            )
        cos, sin = cosine[here, :], sine[here, :]

        def turn(x):
            return x * cos + pltpu.roll(x, HEAD // 2, 1) * sin

        size = length[n]
        live = lax.broadcasted_iota(jnp.int32, (span_size, HEAD), 0) < size
        key = jnp.where(live, turn(projected[:, QC : QC + HEAD]), 0.0).astype(jnp.bfloat16)
        value = jnp.where(live, projected[:, QC + HEAD :], 0.0).astype(jnp.bfloat16)
        keys[here, :] = key
        values[here, :] = value
        row = lax.broadcasted_iota(jnp.int32, (span_size, span_size), 0)
        column = lax.broadcasted_iota(jnp.int32, (span_size, span_size), 1)
        allowed = jnp.logical_and(column <= row, column < size)
        for g in range(GROUPS):
            query = turn(projected[:, g * HEAD : (g + 1) * HEAD]).astype(jnp.bfloat16)
            scores = lax.dot_general(
                query, key, (((1,), (1,)), ((), ())), preferred_element_type=jnp.float32
            ) * scale
            scores = jnp.where(allowed, scores, -1e30)
            raised = jnp.exp(scores - jnp.max(scores, axis=-1, keepdims=True))
            probs = (raised / jnp.sum(raised, axis=-1, keepdims=True)).astype(jnp.bfloat16)
            own[here, g * HEAD : (g + 1) * HEAD] = jnp.dot(
                probs, value, preferred_element_type=jnp.float32
            ).astype(jnp.bfloat16)
        send_own(own, gathered, g_send, g_recv, g_own, n)

        @pl.when(n >= 1)
        def _():
            relay(gathered, g_send, g_recv, n - 1, pieces)

        @pl.when(n >= 2)
        def _():
            relay_far(gathered, g_send, g_recv, n - 2)

        return carry

    half_way = pieces // 2
    lax.fori_loop(0, half_way, one_span, 0)
    for c in range(G // 2):
        forward(wo, zo_send, zo_recv, 1, c)
    lax.fori_loop(half_way, pieces, one_span, 0)
    for p in range(inner):
        for stage, target, ss, rs in (
            (keys, key_out, k_send, k_recv),
            (values, value_out, v_send, v_recv),
        ):
            near, far = chunk_copy(stage, target, ss, rs, p)
            pl.when(i == p)(near.start)
            pl.when(i != p)(far.start)
    relay(gathered, g_send, g_recv, pieces - 1, pieces)
    relay_far(gathered, g_send, g_recv, pieces - 2)
    for s in range(2, line_size - 1):
        for c in range(G // 2):
            forward(wo, zo_send, zo_recv, s, c)
    relay_far(gathered, g_send, g_recv, pieces - 1)

    def fetch(n):
        return pltpu.make_async_copy(
            gathered.at[:, pl.ds(pl.multiple_of(n * span_size, span_size), span_size), :],
            buffer.at[n % 2],
            load.at[n % 2],
        )

    def deliver(n):
        p, part = lax.div(n, spans), n % spans
        src = mine(result, n)
        dst = out.at[
            pl.ds(pl.multiple_of(part * span_size, span_size), span_size),
            pl.ds(pl.multiple_of(i * QC, HEAD), QC),
        ]
        return (
            p,
            pltpu.make_async_copy(src, dst, r_send.at[n]),
            remote(src, dst, r_send.at[n], r_recv.at[i, part], (o * inner + p, t)),
        )

    settle(own, gathered, g_send, g_recv, g_own, 0)
    fetch(0).start()
    for c in range(G // 2):
        forward(wo, zo_send, zo_recv, line_size - 1, c)

    def one_tile(n, carry):
        @pl.when(n + 1 < pieces)
        def _():
            settle(own, gathered, g_send, g_recv, g_own, n + 1)
            fetch(n + 1).start()

        fetch(n).wait()
        total = jnp.zeros((span_size, QC), jnp.float32)
        for m in range(G):
            head = (m % slices) * inner + m // slices
            total = total + jnp.dot(
                buffer[n % 2, m], wo[pl.ds(head * QC, QC), :], preferred_element_type=jnp.float32
            )
        result[pl.ds(pl.multiple_of(n * span_size, span_size), span_size), :] = total.astype(
            jnp.bfloat16
        )
        p, near, far = deliver(n)
        pl.when(i == p)(near.start)
        pl.when(i != p)(far.start)
        return carry

    lax.fori_loop(0, pieces, one_tile, 0)

    hops_sent(wq, zq_send, zq_recv)
    hops_sent(wo, zo_send, zo_recv)
    for d in range(1, G):
        trade(joined, wq, a_send, a_recv, d).wait_send()
        trade(outs, wo, b_send, b_recv, d).wait_send()
    for n in range(spans):
        sent(tokens, t_send, t_recv, n)

    def last(n, carry):
        sent(gathered, g_send, g_recv, n)
        p, near, far = deliver(n)
        pl.when(i == p)(near.wait)
        pl.when(i != p)(far.wait_send)
        return carry

    lax.fori_loop(0, pieces, last, 0)
    for p in range(inner):
        for stage, target, ss, rs in (
            (keys, key_out, k_send, k_recv),
            (values, value_out, v_send, v_recv),
        ):
            near, far = chunk_copy(stage, target, ss, rs, p)
            pl.when(i == p)(near.wait)

            @pl.when(i != p)
            def _():
                far.wait_send()
                chunk_arrived(stage, target, ss, rs, p)

        @pl.when(i != p)
        def _():
            for part in range(spans):
                dst = out.at[pl.ds(part * span_size, span_size), pl.ds(p * QC, QC)]
                remote(
                    mine(result, 0), dst, r_send.at[0], r_recv.at[p, part], (o * inner + p, t)
                ).wait_recv()


def fused(members, slices, spans, span_size, normed, joined, outs, bias, cosine, sine, length):
    inner = G // slices
    line_size = members // inner
    token_rows, features = normed.shape
    rows = joined.shape[1]
    depth = members * slices * rows
    every = inner * token_rows
    pieces = inner * spans
    bf16 = jnp.bfloat16
    dma = pltpu.SemaphoreType.DMA
    hops = [dma((2, line_size, G // 2)), dma((line_size, G // 2))]
    anywhere = pl.BlockSpec(memory_space=pl.ANY)
    vmem = pl.BlockSpec(memory_space=pltpu.VMEM)
    return pl.pallas_call(
        functools.partial(body, members, slices, spans, span_size),
        out_shape=[
            jax.ShapeDtypeStruct((token_rows, inner * QC), bf16),
            jax.ShapeDtypeStruct((token_rows, inner * HEAD), bf16),
            jax.ShapeDtypeStruct((token_rows, inner * HEAD), bf16),
            jax.ShapeDtypeStruct((G, every, QC), bf16),
        ],
        in_specs=[anywhere] * 3 + [vmem] * 3 + [pl.BlockSpec(memory_space=pltpu.SMEM)],
        out_specs=[anywhere] * 4,
        scratch_shapes=[
            pltpu.VMEM((depth, QC + 2 * HEAD), bf16),
            pltpu.VMEM((depth, QC), bf16),
            pltpu.VMEM((G, token_rows, features), bf16),
            pltpu.VMEM((every, QC), bf16),
            pltpu.VMEM((every, HEAD), bf16),
            pltpu.VMEM((every, HEAD), bf16),
            pltpu.VMEM((every, QC), bf16),
            pltpu.VMEM((2, G, span_size, QC), bf16),
            dma((G,)), dma((G,)), dma,
            dma((G,)), dma((G,)), dma,
            *hops, *hops,
            dma((7, spans)), dma((7, spans)), dma((spans,)),
            dma((7, pieces)), dma((7, pieces)), dma((pieces,)),
            dma((2,)),
            dma((pieces,)), dma((inner, spans)),
            dma((inner,)), dma((inner,)),
            dma((inner,)), dma((inner,)),
        ],
        compiler_params=pltpu.CompilerParams(
            collective_id=0, has_side_effects=True, vmem_limit_bytes=61 * 1024 * 1024
        ),
    )(normed, joined, outs, bias, cosine, sine, length)


def local(
    hidden_in,
    norm_gain,
    query_weight,
    key_weight,
    value_weight,
    out_weight,
    query_bias,
    key_bias,
    value_bias,
    span_start,
    span_length,
):
    slices = lax.axis_size("tensor")
    members = lax.axis_size("fsdp")
    devices = slices * members
    inner = KV_HEADS // slices
    outer = devices // KV_HEADS
    line = lax.axis_index("fsdp") // inner
    i = lax.axis_index("fsdp") % inner
    t = lax.axis_index("tensor")
    token_rows, features = hidden_in.shape
    local_spans = span_start.shape[0]
    span_size = token_rows // local_spans
    learner_rows = query_weight.shape[0]
    qc = GROUPS * HEAD
    oc = out_weight.shape[1] // KV_HEADS

    def xor(x, k):
        return lax.ppermute(x, AXES, [(d, d ^ k) for d in range(devices)])

    def shift(x, step):
        pairs = [
            (d, d + step * KV_HEADS)
            for d in range(devices)
            if 0 <= d + step * KV_HEADS < devices
        ]
        return lax.ppermute(x, AXES, pairs)

    def gather_group(own):
        half = own.shape[0] // 2
        one = xor(own, 1)
        four = xor(own, 4)
        five = jnp.concatenate([xor(four[:half], 1), xor(one[half:], 4)], axis=0)
        got = {0: own, 1: one, 4: four, 5: five}
        for k in (0, 1, 4, 5):
            got[k ^ 2] = xor(got[k], 2)
        return [got[k] for k in range(KV_HEADS)]

    def blocks(weight):
        cols = weight.shape[1] // KV_HEADS
        cut = weight.reshape(learner_rows, slices, inner, cols)
        return jnp.transpose(cut, (2, 1, 0, 3)).reshape(KV_HEADS, learner_rows, cols)

    def exchange(stacked):
        groups = [[g * KV_HEADS + j for j in range(KV_HEADS)] for g in range(outer)]
        arrived = lax.all_to_all(
            stacked, AXES, split_axis=0, concat_axis=0, axis_index_groups=groups, tiled=True
        )
        return arrived.reshape(KV_HEADS * learner_rows, stacked.shape[2])

    def gather_line(slab):
        below, above = [], []
        up = down = slab
        for _ in range(outer - 1):
            up = shift(up, 1)
            down = shift(down, -1)
            below.append(up)
            above.append(down)
        every = jnp.stack(below[::-1] + [slab] + above)
        whole = lax.dynamic_slice_in_dim(every, outer - 1 - line, outer, axis=0)
        return whole.reshape(outer * slab.shape[0], slab.shape[1])

    def unswap(parts):
        parts = list(parts)
        bit = 1
        while bit < inner:
            flip = (i & bit) != 0
            parts = [jnp.where(flip, parts[p ^ bit], parts[p]) for p in range(inner)]
            bit *= 2
        return parts

    joined = jnp.concatenate(
        [blocks(query_weight), blocks(key_weight), blocks(value_weight)], axis=2
    )
    out_blocks = blocks(out_weight)
    source = hidden_in.astype(jnp.float32)
    squares = jnp.sum(source * source, axis=-1, keepdims=True)
    bit = 1
    while bit < slices:
        squares = squares + xor(squares, bit)
        bit *= 2
    inverse_rms = lax.rsqrt(squares / (features * slices) + epsilon)
    gain = lax.dynamic_slice_in_dim(norm_gain, t * features, features).astype(jnp.float32)
    normed = (source * inverse_rms * gain).astype(jnp.bfloat16)
    bias = jnp.concatenate(
        [
            lax.dynamic_slice_in_dim(query_bias, i * qc, qc),
            lax.dynamic_slice_in_dim(key_bias, i * HEAD, HEAD),
            lax.dynamic_slice_in_dim(value_bias, i * HEAD, HEAD),
        ]
    ).astype(jnp.float32)
    marks = jnp.stack([span_start, span_length])
    marks = [marks] + [xor(marks, ki * slices) for ki in range(1, inner)]
    if learner_rows % 16 == 0 and outer >= 3:
        marks = jnp.concatenate(unswap(marks), axis=1)
        cosine, sine = angles(marks[0], span_size)
        cosine, sine = cosine[:, 0], sine[:, 0]
        return tuple(
            fused(
                members, slices, local_spans, span_size, normed, joined, out_blocks,
                bias[None, :],
                jnp.concatenate([cosine, cosine], axis=1),
                jnp.concatenate([-sine, sine], axis=1),
                marks[1],
            )[:3]
        )

    tokens = gather_group(normed)
    weight = gather_line(exchange(joined))
    out_whole = gather_line(exchange(out_blocks))
    rows = jnp.arange(span_size, dtype=jnp.int32)[:, None]
    columns = jnp.arange(span_size, dtype=jnp.int32)[None, :]
    halves = [
        lax.dynamic_slice_in_dim(weight, (t ^ kt) * features, features) for kt in range(slices)
    ]
    mixes, key_parts, value_parts = [], [], []
    for ki in range(inner):
        projected = bias[None, :]
        for kt in range(slices):
            projected = projected + jnp.dot(
                tokens[ki * slices + kt], halves[kt], preferred_element_type=jnp.float32
            )
        start, length = marks[ki][0], marks[ki][1]
        cosine, sine = angles(start, span_size)
        query = rotate(
            projected[:, :qc].reshape(token_rows, GROUPS, HEAD), cosine, sine
        ).astype(jnp.bfloat16)
        keys = rotate(projected[:, None, qc : qc + HEAD], cosine, sine)[:, 0]
        live = (columns < length[:, None]).reshape(token_rows, 1)
        key_cache = jnp.where(live, keys, 0.0).astype(jnp.bfloat16)
        value_cache = jnp.where(live, projected[:, qc + HEAD :], 0.0).astype(jnp.bfloat16)
        query_blocks = query.reshape(local_spans, span_size, GROUPS, HEAD)
        key_blocks = key_cache.reshape(local_spans, span_size, HEAD)
        value_blocks = value_cache.reshape(local_spans, span_size, HEAD)
        scores = jnp.einsum(
            "sqgd,std->sgqt", query_blocks, key_blocks, preferred_element_type=jnp.float32
        ) * HEAD ** (-0.5)
        allowed = (columns <= rows)[None] & (columns[None] < length[:, None, None])
        scores = jnp.where(allowed[:, None], scores, -1e30)
        highest = jnp.max(scores, axis=-1, keepdims=True)
        raised = jnp.exp(scores - highest)
        probs = (raised / jnp.sum(raised, axis=-1, keepdims=True)).astype(jnp.bfloat16)
        mixed = jnp.einsum(
            "sgqt,std->sqgd", probs, value_blocks, preferred_element_type=jnp.float32
        )
        mixes.append(mixed.reshape(token_rows, qc).astype(jnp.bfloat16))
        key_parts.append(key_cache if ki == 0 else xor(key_cache, ki * slices))
        value_parts.append(value_cache if ki == 0 else xor(value_cache, ki * slices))

    mixes = unswap(mixes)
    attended = gather_group(jnp.concatenate(mixes, axis=0))
    combined = 0.0
    for k in range(KV_HEADS):
        head = (t ^ (k % slices)) * inner + (i ^ (k // slices))
        combined = combined + jnp.dot(
            attended[k],
            lax.dynamic_slice_in_dim(out_whole, head * qc, qc),
            preferred_element_type=jnp.float32,
        )
    result = combined.astype(jnp.bfloat16).reshape(inner, token_rows, oc)
    result = unswap([result[p] for p in range(inner)])
    out_parts = [result[0]] + [xor(result[ki], ki * slices) for ki in range(1, inner)]
    return tuple(
        jnp.concatenate(unswap(parts), axis=1)
        for parts in (out_parts, key_parts, value_parts)
    )


def solution(mesh):
    placed = (
        P("fsdp", "tensor"),
        P(),
        P(("fsdp", "tensor"), None),
        P(("fsdp", "tensor"), None),
        P(("fsdp", "tensor"), None),
        P(("fsdp", "tensor"), None),
        P("tensor"),
        P("tensor"),
        P("tensor"),
        P("fsdp"),
        P("fsdp"),
    )
    return jax.shard_map(
        local,
        mesh=mesh,
        in_specs=placed,
        out_specs=(P("fsdp", "tensor"), P("fsdp", "tensor"), P("fsdp", "tensor")),
        check_vma=False,
    )
```

```python
import functools

import jax
import jax.numpy as jnp
from jax import lax
from jax.experimental import pallas as pl
from jax.experimental.pallas import tpu as pltpu
from jax.sharding import PartitionSpec as P

HEADS = 40
KV_HEADS = 8
HEAD = 128
GROUPS = HEADS // KV_HEADS
AXES = ("fsdp", "tensor")

rope_base = 1000000.0
epsilon = 1e-06


def rotate(entries, cosine, sine):
    half = entries.shape[-1] // 2
    first = entries[..., :half]
    second = entries[..., half:]
    return jnp.concatenate(
        [first * cosine - second * sine, second * cosine + first * sine], axis=-1
    )


def angles(span_start, span_size):
    positions = span_start[:, None] + jnp.arange(span_size, dtype=jnp.int32)[None, :]
    inverse = 1.0 / rope_base ** (jnp.arange(0, HEAD, 2, dtype=jnp.float32) / HEAD)
    phase = positions.reshape(-1).astype(jnp.float32)[:, None] * inverse[None, :]
    return (jnp.cos(phase)[:, None, :], jnp.sin(phase)[:, None, :])


MESH = pl.DeviceIdType.MESH
G = KV_HEADS
QC = GROUPS * HEAD


def flip(m, bit):
    return m + bit - 2 * bit * (lax.div(m, bit) % 2)


def body(
    members, slices, spans, span_size,
    normed, query_in, key_in, value_in, out_in, bias, cosine, sine, length,
    out, key_out, value_out, gathered,
    wq, wo, tokens, own, keys, values, result, buffer,
    a_send, a_recv, a_own, b_send, b_recv, b_own,
    zq_send, zq_recv, zo_send, zo_recv,
    t_send, t_recv, t_own, g_send, g_recv, g_own,
    load, r_send, r_recv, k_send, k_recv, v_send, v_recv,
):
    inner = G // slices
    line_size = members // inner
    f = lax.axis_index("fsdp")
    t = lax.axis_index("tensor")
    o = lax.div(f, inner)
    i = f % inner
    me = i * slices + t
    rows = query_in.shape[0]
    mx, my, mc = flip(me, 4), flip(me, 1), flip(me, 2)
    md = flip(mx, 1)

    def member(m):
        return (o * inner + lax.div(m, slices), m % slices)

    def remote(src, dst, ss, rs, where):
        return pltpu.make_async_remote_copy(
            src_ref=src, dst_ref=dst, send_sem=ss, recv_sem=rs, device_id=where, device_id_type=MESH
        )

    barrier = pltpu.get_barrier_semaphore()
    for d in range(1, G):
        pl.semaphore_signal(
            barrier, inc=1, device_id=member((me + d) % G), device_id_type=MESH
        )

    @pl.when(o > 0)
    def _():
        pl.semaphore_signal(barrier, inc=1, device_id=(f - inner, t), device_id_type=MESH)

    @pl.when(o < line_size - 1)
    def _():
        pl.semaphore_signal(barrier, inc=1, device_id=(f + inner, t), device_id_type=MESH)

    ends = (o == 0).astype(jnp.int32) + (o == line_size - 1).astype(jnp.int32)
    pl.semaphore_wait(barrier, G + 1 - ends)

    def place(buf, origin, m, count):
        return buf.at[pl.ds(pl.multiple_of((origin * G + m) * rows, rows), count * rows), :]

    def cut(src, m):
        cols = src.shape[1] // G
        head = (m % slices) * inner + lax.div(m, slices)
        return src.at[:, pl.ds(pl.multiple_of(head * cols, HEAD), cols)]

    def lanes(buf, m, at, cols):
        return place(buf, o, m, 1).at[:, pl.ds(at, cols)]

    def trade(part, buf, ss, rs, d):
        k, src, at = part
        to = (me + d) % G
        dst = lanes(buf, me, at, src.shape[1] // G)
        return remote(cut(src, to), dst, ss.at[k, d], rs.at[k, d], member(to))

    def trade_own(part, buf, sem):
        k, src, at = part
        dst = lanes(buf, me, at, src.shape[1] // G)
        return pltpu.make_async_copy(cut(src, me), dst, sem.at[k])

    def trade_start(parts, buf, ss, rs, sem):
        for d in range(1, G):
            for part in parts:
                trade(part, buf, ss, rs, d).start()
        for part in parts:
            trade_own(part, buf, sem).start()

    def trade_wait(parts, buf, ss, rs, sem, m):
        @pl.when(m == me)
        def _():
            for part in parts:
                trade_own(part, buf, sem).wait()

        @pl.when(m != me)
        def _():
            d = (me - m + G) % G
            for k, src, at in parts:
                here = lanes(buf, m, at, src.shape[1] // G)
                remote(here, here, ss.at[k, d], rs.at[k, d], member(m)).wait_recv()

    inputs = ((0, query_in, 0), (1, key_in, QC), (2, value_in, QC + HEAD))
    outs = ((0, out_in, 0),)

    def hop(buf, ss, rs, origin, c, way):
        here = place(buf, origin, 2 * c, 2)
        way_f = f + inner if way == 0 else f - inner
        return remote(here, here, ss.at[way, origin, c], rs.at[origin, c], (way_f, t))

    def forward(buf, ss, rs, s, c):
        below, above = o - s, o + s
        if not isinstance(s, int) or s > 0:
            @pl.when(below >= 0)
            def _():
                hop(buf, ss, rs, below, c, 0).wait_recv()

            @pl.when(above < line_size)
            def _():
                hop(buf, ss, rs, above, c, 0).wait_recv()

        @pl.when(jnp.logical_and(below >= 0, o < line_size - 1))
        def _():
            hop(buf, ss, rs, below, c, 0).start()

        @pl.when(jnp.logical_and(above < line_size, o > 0))
        def _():
            hop(buf, ss, rs, above, c, 1).start()

    def hops_sent(buf, ss, rs, s):
        below, above = o - s, o + s
        for c in range(G // 2):
            hop_sent(buf, ss, rs, below, above, c)

    def hop_sent(buf, ss, rs, below, above, c):
        @pl.when(jnp.logical_and(below >= 0, o < line_size - 1))
        def _():
            hop(buf, ss, rs, below, c, 0).wait_send()

        @pl.when(jnp.logical_and(above < line_size, o > 0))
        def _():
            hop(buf, ss, rs, above, c, 1).wait_send()

    def piece(buf, m, n):
        return buf.at[m, pl.ds(pl.multiple_of(n * span_size, span_size), span_size), :]

    def mine(src, n):
        return src.at[pl.ds(pl.multiple_of(n * span_size, span_size), span_size), :]

    def send_own(src, buf, ss, rs, sem, n):
        for kind, to in ((0, mx), (1, my), (2, mc)):
            remote(
                mine(src, n), piece(buf, me, n), ss.at[kind, n], rs.at[kind, n], member(to)
            ).start()
        pltpu.make_async_copy(mine(src, n), piece(buf, me, n), sem.at[n]).start()

    def arrived(buf, ss, rs, kind, slot, n):
        here = piece(buf, slot, n)
        remote(here, here, ss.at[kind, n], rs.at[kind, n], member(mx)).wait_recv()

    def pass_on(buf, ss, rs, kind, slot, to, n):
        here = piece(buf, slot, n)
        remote(here, here, ss.at[kind, n], rs.at[kind, n], member(to)).start()

    def relay(buf, ss, rs, n, total):
        arrived(buf, ss, rs, 0, mx, n)
        arrived(buf, ss, rs, 1, my, n)

        @pl.when(n < total // 2)
        def _():
            pass_on(buf, ss, rs, 3, mx, my, n)

        @pl.when(n >= total // 2)
        def _():
            pass_on(buf, ss, rs, 3, my, mx, n)

        pass_on(buf, ss, rs, 4, mx, mc, n)
        pass_on(buf, ss, rs, 5, my, mc, n)

    def relay_far(buf, ss, rs, n):
        arrived(buf, ss, rs, 3, md, n)
        pass_on(buf, ss, rs, 6, md, mc, n)

    def settle(src, buf, ss, rs, sem, n):
        pltpu.make_async_copy(mine(src, n), piece(buf, me, n), sem.at[n]).wait()
        for kind, slot in ((2, mc), (4, flip(mx, 2)), (5, flip(my, 2)), (6, flip(md, 2))):
            arrived(buf, ss, rs, kind, slot, n)

    def sent(buf, ss, rs, n):
        for kind in range(7):
            here = piece(buf, me, n)
            remote(here, here, ss.at[kind, n], rs.at[kind, n], member(mx)).wait_send()

    trade_start(inputs, wq, a_send, a_recv, a_own)
    for n in range(spans):
        send_own(normed, tokens, t_send, t_recv, t_own, n)
    for c in range(G // 2):
        for m in (2 * c, 2 * c + 1):
            trade_wait(inputs, wq, a_send, a_recv, a_own, m)
        forward(wq, zq_send, zq_recv, 0, c)
    for c in range(G // 2):
        forward(wq, zq_send, zq_recv, 1, c)
    for n in range(spans):
        relay(tokens, t_send, t_recv, n, spans)
    trade_start(outs, wo, b_send, b_recv, b_own)
    for s in range(2, line_size - 1):
        for c in range(G // 2):
            forward(wq, zq_send, zq_recv, s, c)
    for n in range(spans):
        relay_far(tokens, t_send, t_recv, n)
    for m in range(G):
        trade_wait(outs, wo, b_send, b_recv, b_own, m)
    for c in range(G // 2):
        hop_sent(wq, zq_send, zq_recv, o - (line_size - 2), o + (line_size - 2), c)
        forward(wo, zo_send, zo_recv, 0, c)
    for n in range(spans):
        settle(normed, tokens, t_send, t_recv, t_own, n)
    for c in range(G // 2):
        forward(wq, zq_send, zq_recv, line_size - 1, c)

    pieces = inner * spans
    features = tokens.shape[2]
    scale = HEAD ** (-0.5)

    def chunk_copy(stage, target, ss, rs, p):
        src = stage.at[pl.ds(pl.multiple_of(p * spans * span_size, span_size), spans * span_size), :]
        dst = target.at[:, pl.ds(pl.multiple_of(i * HEAD, HEAD), HEAD)]
        return (
            pltpu.make_async_copy(src, dst, ss.at[p]),
            remote(src, dst, ss.at[p], rs.at[i], (o * inner + p, t)),
        )

    def chunk_arrived(stage, target, ss, rs, p):
        src = stage.at[pl.ds(0, spans * span_size), :]
        dst = target.at[:, pl.ds(pl.multiple_of(p * HEAD, HEAD), HEAD)]
        remote(src, dst, ss.at[p], rs.at[p], (o * inner + p, t)).wait_recv()

    def one_span(n, carry):
        p = lax.div(n, spans)
        part = n % spans
        here = pl.ds(pl.multiple_of(n * span_size, span_size), span_size)
        projected = bias[...]
        for half in range(slices):
            projected = projected + jnp.dot(
                tokens[p * slices + half, pl.ds(pl.multiple_of(part * span_size, span_size), span_size), :],
                wq[pl.ds(half * features, features), :],
                preferred_element_type=jnp.float32,
            )
        cos, sin = cosine[here, :], sine[here, :]

        def turn(x):
            return x * cos + pltpu.roll(x, HEAD // 2, 1) * sin

        size = length[n]
        live = lax.broadcasted_iota(jnp.int32, (span_size, HEAD), 0) < size
        key = jnp.where(live, turn(projected[:, QC : QC + HEAD]), 0.0).astype(jnp.bfloat16)
        value = jnp.where(live, projected[:, QC + HEAD :], 0.0).astype(jnp.bfloat16)
        keys[here, :] = key
        values[here, :] = value
        row = lax.broadcasted_iota(jnp.int32, (span_size, span_size), 0)
        column = lax.broadcasted_iota(jnp.int32, (span_size, span_size), 1)
        allowed = jnp.logical_and(column <= row, column < size)
        for g in range(GROUPS):
            query = turn(projected[:, g * HEAD : (g + 1) * HEAD]).astype(jnp.bfloat16)
            scores = lax.dot_general(
                query, key, (((1,), (1,)), ((), ())), preferred_element_type=jnp.float32
            ) * scale
            scores = jnp.where(allowed, scores, -1e30)
            raised = jnp.exp(scores - jnp.max(scores, axis=-1, keepdims=True))
            probs = (raised / jnp.sum(raised, axis=-1, keepdims=True)).astype(jnp.bfloat16)
            own[here, g * HEAD : (g + 1) * HEAD] = jnp.dot(
                probs, value, preferred_element_type=jnp.float32
            ).astype(jnp.bfloat16)
        send_own(own, gathered, g_send, g_recv, g_own, n)
        forward(wo, zo_send, zo_recv, 1 + lax.div(n, G // 2), n % (G // 2))

        @pl.when(n >= 1)
        def _():
            relay(gathered, g_send, g_recv, n - 1, pieces)

        @pl.when(n >= 2)
        def _():
            relay_far(gathered, g_send, g_recv, n - 2)

        return carry

    lax.fori_loop(0, pieces, one_span, 0)
    for p in range(inner):
        for stage, target, ss, rs in (
            (keys, key_out, k_send, k_recv),
            (values, value_out, v_send, v_recv),
        ):
            near, far = chunk_copy(stage, target, ss, rs, p)
            pl.when(i == p)(near.start)
            pl.when(i != p)(far.start)
    relay(gathered, g_send, g_recv, pieces - 1, pieces)
    relay_far(gathered, g_send, g_recv, pieces - 2)
    relay_far(gathered, g_send, g_recv, pieces - 1)

    def fetch(n):
        return pltpu.make_async_copy(
            gathered.at[:, pl.ds(pl.multiple_of(n * span_size, span_size), span_size), :],
            buffer.at[n % 2],
            load.at[n % 2],
        )

    def deliver(n):
        p, part = lax.div(n, spans), n % spans
        src = mine(result, n)
        dst = out.at[
            pl.ds(pl.multiple_of(part * span_size, span_size), span_size),
            pl.ds(pl.multiple_of(i * QC, HEAD), QC),
        ]
        return (
            p,
            pltpu.make_async_copy(src, dst, r_send.at[n]),
            remote(src, dst, r_send.at[n], r_recv.at[i, part], (o * inner + p, t)),
        )

    settle(own, gathered, g_send, g_recv, g_own, 0)
    fetch(0).start()
    for s in range(1 + pieces // (G // 2), line_size):
        for c in range(G // 2):
            forward(wo, zo_send, zo_recv, s, c)

    def one_tile(n, carry):
        @pl.when(n + 1 < pieces)
        def _():
            settle(own, gathered, g_send, g_recv, g_own, n + 1)
            fetch(n + 1).start()

        fetch(n).wait()
        total = jnp.zeros((span_size, QC), jnp.float32)
        for m in range(G):
            head = (m % slices) * inner + m // slices
            total = total + jnp.dot(
                buffer[n % 2, m], wo[pl.ds(head * QC, QC), :], preferred_element_type=jnp.float32
            )
        result[pl.ds(pl.multiple_of(n * span_size, span_size), span_size), :] = total.astype(
            jnp.bfloat16
        )
        p, near, far = deliver(n)
        pl.when(i == p)(near.start)
        pl.when(i != p)(far.start)
        return carry

    lax.fori_loop(0, pieces, one_tile, 0)

    for s in range(line_size):
        if s != line_size - 2:
            hops_sent(wq, zq_send, zq_recv, s)
        hops_sent(wo, zo_send, zo_recv, s)
    for d in range(1, G):
        for part in inputs:
            trade(part, wq, a_send, a_recv, d).wait_send()
        for part in outs:
            trade(part, wo, b_send, b_recv, d).wait_send()
    for n in range(spans):
        sent(tokens, t_send, t_recv, n)

    def last(n, carry):
        sent(gathered, g_send, g_recv, n)
        p, near, far = deliver(n)
        pl.when(i == p)(near.wait)
        pl.when(i != p)(far.wait_send)
        return carry

    lax.fori_loop(0, pieces, last, 0)
    for p in range(inner):
        for stage, target, ss, rs in (
            (keys, key_out, k_send, k_recv),
            (values, value_out, v_send, v_recv),
        ):
            near, far = chunk_copy(stage, target, ss, rs, p)
            pl.when(i == p)(near.wait)

            @pl.when(i != p)
            def _():
                far.wait_send()
                chunk_arrived(stage, target, ss, rs, p)

        @pl.when(i != p)
        def _():
            for part in range(spans):
                dst = out.at[pl.ds(part * span_size, span_size), pl.ds(p * QC, QC)]
                remote(
                    mine(result, 0), dst, r_send.at[0], r_recv.at[p, part], (o * inner + p, t)
                ).wait_recv()


def fused(members, slices, spans, span_size, normed, weights, bias, cosine, sine, length):
    inner = G // slices
    line_size = members // inner
    token_rows, features = normed.shape
    rows = weights[0].shape[0]
    depth = members * slices * rows
    every = inner * token_rows
    pieces = inner * spans
    bf16 = jnp.bfloat16
    dma = pltpu.SemaphoreType.DMA
    hops = [dma((2, line_size, G // 2)), dma((line_size, G // 2))]
    anywhere = pl.BlockSpec(memory_space=pl.ANY)
    vmem = pl.BlockSpec(memory_space=pltpu.VMEM)
    return pl.pallas_call(
        functools.partial(body, members, slices, spans, span_size),
        out_shape=[
            jax.ShapeDtypeStruct((token_rows, inner * QC), bf16),
            jax.ShapeDtypeStruct((token_rows, inner * HEAD), bf16),
            jax.ShapeDtypeStruct((token_rows, inner * HEAD), bf16),
            jax.ShapeDtypeStruct((G, every, QC), bf16),
        ],
        in_specs=[anywhere] * 5 + [vmem] * 3 + [pl.BlockSpec(memory_space=pltpu.SMEM)],
        out_specs=[anywhere] * 4,
        scratch_shapes=[
            pltpu.VMEM((depth, QC + 2 * HEAD), bf16),
            pltpu.VMEM((depth, QC), bf16),
            pltpu.VMEM((G, token_rows, features), bf16),
            pltpu.VMEM((every, QC), bf16),
            pltpu.VMEM((every, HEAD), bf16),
            pltpu.VMEM((every, HEAD), bf16),
            pltpu.VMEM((every, QC), bf16),
            pltpu.VMEM((2, G, span_size, QC), bf16),
            dma((3, G)), dma((3, G)), dma((3,)),
            dma((1, G)), dma((1, G)), dma((1,)),
            *hops, *hops,
            dma((7, spans)), dma((7, spans)), dma((spans,)),
            dma((7, pieces)), dma((7, pieces)), dma((pieces,)),
            dma((2,)),
            dma((pieces,)), dma((inner, spans)),
            dma((inner,)), dma((inner,)),
            dma((inner,)), dma((inner,)),
        ],
        compiler_params=pltpu.CompilerParams(
            collective_id=0, has_side_effects=True, vmem_limit_bytes=61 * 1024 * 1024
        ),
    )(normed, *weights, bias, cosine, sine, length)


def local(
    hidden_in,
    norm_gain,
    query_weight,
    key_weight,
    value_weight,
    out_weight,
    query_bias,
    key_bias,
    value_bias,
    span_start,
    span_length,
):
    slices = lax.axis_size("tensor")
    members = lax.axis_size("fsdp")
    devices = slices * members
    inner = KV_HEADS // slices
    outer = devices // KV_HEADS
    line = lax.axis_index("fsdp") // inner
    i = lax.axis_index("fsdp") % inner
    t = lax.axis_index("tensor")
    token_rows, features = hidden_in.shape
    local_spans = span_start.shape[0]
    span_size = token_rows // local_spans
    learner_rows = query_weight.shape[0]
    qc = GROUPS * HEAD
    oc = out_weight.shape[1] // KV_HEADS

    def xor(x, k):
        return lax.ppermute(x, AXES, [(d, d ^ k) for d in range(devices)])

    def shift(x, step):
        pairs = [
            (d, d + step * KV_HEADS)
            for d in range(devices)
            if 0 <= d + step * KV_HEADS < devices
        ]
        return lax.ppermute(x, AXES, pairs)

    def gather_group(own):
        half = own.shape[0] // 2
        one = xor(own, 1)
        four = xor(own, 4)
        five = jnp.concatenate([xor(four[:half], 1), xor(one[half:], 4)], axis=0)
        got = {0: own, 1: one, 4: four, 5: five}
        for k in (0, 1, 4, 5):
            got[k ^ 2] = xor(got[k], 2)
        return [got[k] for k in range(KV_HEADS)]

    def blocks(weight):
        cols = weight.shape[1] // KV_HEADS
        cut = weight.reshape(learner_rows, slices, inner, cols)
        return jnp.transpose(cut, (2, 1, 0, 3)).reshape(KV_HEADS, learner_rows, cols)

    def exchange(stacked):
        groups = [[g * KV_HEADS + j for j in range(KV_HEADS)] for g in range(outer)]
        arrived = lax.all_to_all(
            stacked, AXES, split_axis=0, concat_axis=0, axis_index_groups=groups, tiled=True
        )
        return arrived.reshape(KV_HEADS * learner_rows, stacked.shape[2])

    def gather_line(slab):
        below, above = [], []
        up = down = slab
        for _ in range(outer - 1):
            up = shift(up, 1)
            down = shift(down, -1)
            below.append(up)
            above.append(down)
        every = jnp.stack(below[::-1] + [slab] + above)
        whole = lax.dynamic_slice_in_dim(every, outer - 1 - line, outer, axis=0)
        return whole.reshape(outer * slab.shape[0], slab.shape[1])

    def unswap(parts):
        parts = list(parts)
        bit = 1
        while bit < inner:
            flip = (i & bit) != 0
            parts = [jnp.where(flip, parts[p ^ bit], parts[p]) for p in range(inner)]
            bit *= 2
        return parts

    joined = jnp.concatenate(
        [blocks(query_weight), blocks(key_weight), blocks(value_weight)], axis=2
    )
    out_blocks = blocks(out_weight)
    source = hidden_in.astype(jnp.float32)
    squares = jnp.sum(source * source, axis=-1, keepdims=True)
    bit = 1
    while bit < slices:
        squares = squares + xor(squares, bit)
        bit *= 2
    inverse_rms = lax.rsqrt(squares / (features * slices) + epsilon)
    gain = lax.dynamic_slice_in_dim(norm_gain, t * features, features).astype(jnp.float32)
    normed = (source * inverse_rms * gain).astype(jnp.bfloat16)
    bias = jnp.concatenate(
        [
            lax.dynamic_slice_in_dim(query_bias, i * qc, qc),
            lax.dynamic_slice_in_dim(key_bias, i * HEAD, HEAD),
            lax.dynamic_slice_in_dim(value_bias, i * HEAD, HEAD),
        ]
    ).astype(jnp.float32)
    marks = jnp.stack([span_start, span_length])
    marks = [marks] + [xor(marks, ki * slices) for ki in range(1, inner)]
    if learner_rows % 16 == 0 and outer >= 3:
        marks = jnp.concatenate(unswap(marks), axis=1)
        cosine, sine = angles(marks[0], span_size)
        cosine, sine = cosine[:, 0], sine[:, 0]
        return tuple(
            fused(
                members, slices, local_spans, span_size, normed,
                (query_weight, key_weight, value_weight, out_weight),
                bias[None, :],
                jnp.concatenate([cosine, cosine], axis=1),
                jnp.concatenate([-sine, sine], axis=1),
                marks[1],
            )[:3]
        )

    tokens = gather_group(normed)
    weight = gather_line(exchange(joined))
    out_whole = gather_line(exchange(out_blocks))
    rows = jnp.arange(span_size, dtype=jnp.int32)[:, None]
    columns = jnp.arange(span_size, dtype=jnp.int32)[None, :]
    halves = [
        lax.dynamic_slice_in_dim(weight, (t ^ kt) * features, features) for kt in range(slices)
    ]
    mixes, key_parts, value_parts = [], [], []
    for ki in range(inner):
        projected = bias[None, :]
        for kt in range(slices):
            projected = projected + jnp.dot(
                tokens[ki * slices + kt], halves[kt], preferred_element_type=jnp.float32
            )
        start, length = marks[ki][0], marks[ki][1]
        cosine, sine = angles(start, span_size)
        query = rotate(
            projected[:, :qc].reshape(token_rows, GROUPS, HEAD), cosine, sine
        ).astype(jnp.bfloat16)
        keys = rotate(projected[:, None, qc : qc + HEAD], cosine, sine)[:, 0]
        live = (columns < length[:, None]).reshape(token_rows, 1)
        key_cache = jnp.where(live, keys, 0.0).astype(jnp.bfloat16)
        value_cache = jnp.where(live, projected[:, qc + HEAD :], 0.0).astype(jnp.bfloat16)
        query_blocks = query.reshape(local_spans, span_size, GROUPS, HEAD)
        key_blocks = key_cache.reshape(local_spans, span_size, HEAD)
        value_blocks = value_cache.reshape(local_spans, span_size, HEAD)
        scores = jnp.einsum(
            "sqgd,std->sgqt", query_blocks, key_blocks, preferred_element_type=jnp.float32
        ) * HEAD ** (-0.5)
        allowed = (columns <= rows)[None] & (columns[None] < length[:, None, None])
        scores = jnp.where(allowed[:, None], scores, -1e30)
        highest = jnp.max(scores, axis=-1, keepdims=True)
        raised = jnp.exp(scores - highest)
        probs = (raised / jnp.sum(raised, axis=-1, keepdims=True)).astype(jnp.bfloat16)
        mixed = jnp.einsum(
            "sgqt,std->sqgd", probs, value_blocks, preferred_element_type=jnp.float32
        )
        mixes.append(mixed.reshape(token_rows, qc).astype(jnp.bfloat16))
        key_parts.append(key_cache if ki == 0 else xor(key_cache, ki * slices))
        value_parts.append(value_cache if ki == 0 else xor(value_cache, ki * slices))

    mixes = unswap(mixes)
    attended = gather_group(jnp.concatenate(mixes, axis=0))
    combined = 0.0
    for k in range(KV_HEADS):
        head = (t ^ (k % slices)) * inner + (i ^ (k // slices))
        combined = combined + jnp.dot(
            attended[k],
            lax.dynamic_slice_in_dim(out_whole, head * qc, qc),
            preferred_element_type=jnp.float32,
        )
    result = combined.astype(jnp.bfloat16).reshape(inner, token_rows, oc)
    result = unswap([result[p] for p in range(inner)])
    out_parts = [result[0]] + [xor(result[ki], ki * slices) for ki in range(1, inner)]
    return tuple(
        jnp.concatenate(unswap(parts), axis=1)
        for parts in (out_parts, key_parts, value_parts)
    )


def solution(mesh):
    placed = (
        P("fsdp", "tensor"),
        P(),
        P(("fsdp", "tensor"), None),
        P(("fsdp", "tensor"), None),
        P(("fsdp", "tensor"), None),
        P(("fsdp", "tensor"), None),
        P("tensor"),
        P("tensor"),
        P("tensor"),
        P("fsdp"),
        P("fsdp"),
    )
    return jax.shard_map(
        local,
        mesh=mesh,
        in_specs=placed,
        out_specs=(P("fsdp", "tensor"), P("fsdp", "tensor"), P("fsdp", "tensor")),
        check_vma=False,
    )
```

```python
import functools

import jax
import jax.numpy as jnp
from jax import lax
from jax.experimental import pallas as pl
from jax.experimental.pallas import tpu as pltpu
from jax.sharding import PartitionSpec as P

HEADS = 40
KV_HEADS = 8
HEAD = 128
GROUPS = HEADS // KV_HEADS
AXES = ("fsdp", "tensor")

rope_base = 1000000.0
epsilon = 1e-06


def rotate(entries, cosine, sine):
    half = entries.shape[-1] // 2
    first = entries[..., :half]
    second = entries[..., half:]
    return jnp.concatenate(
        [first * cosine - second * sine, second * cosine + first * sine], axis=-1
    )


def angles(span_start, span_size):
    positions = span_start[:, None] + jnp.arange(span_size, dtype=jnp.int32)[None, :]
    inverse = 1.0 / rope_base ** (jnp.arange(0, HEAD, 2, dtype=jnp.float32) / HEAD)
    phase = positions.reshape(-1).astype(jnp.float32)[:, None] * inverse[None, :]
    return (jnp.cos(phase)[:, None, :], jnp.sin(phase)[:, None, :])


MESH = pl.DeviceIdType.MESH
G = KV_HEADS
QC = GROUPS * HEAD


def flip(m, bit):
    return m + bit - 2 * bit * (lax.div(m, bit) % 2)


def body(
    members, slices, spans, span_size,
    normed, query_in, key_in, value_in, out_in, bias, cosine, sine, length,
    out, key_out, value_out, gathered,
    wq, wo, tokens, own, keys, values, result, buffer, partial,
    a_send, a_recv, a_own, b_send, b_recv, b_own,
    zq_send, zq_recv, zo_send, zo_recv,
    t_send, t_recv, t_own, g_send, g_recv, g_own,
    load, r_send, r_recv, k_send, k_recv, v_send, v_recv,
):
    inner = G // slices
    line_size = members // inner
    f = lax.axis_index("fsdp")
    t = lax.axis_index("tensor")
    o = lax.div(f, inner)
    i = f % inner
    me = i * slices + t
    rows = query_in.shape[0]
    mx, my, mc = flip(me, 4), flip(me, 1), flip(me, 2)
    md = flip(mx, 1)

    def member(m):
        return (o * inner + lax.div(m, slices), m % slices)

    def remote(src, dst, ss, rs, where):
        return pltpu.make_async_remote_copy(
            src_ref=src, dst_ref=dst, send_sem=ss, recv_sem=rs, device_id=where, device_id_type=MESH
        )

    barrier = pltpu.get_barrier_semaphore()
    for d in range(1, G):
        pl.semaphore_signal(
            barrier, inc=1, device_id=member((me + d) % G), device_id_type=MESH
        )

    @pl.when(o > 0)
    def _():
        pl.semaphore_signal(barrier, inc=1, device_id=(f - inner, t), device_id_type=MESH)

    @pl.when(o < line_size - 1)
    def _():
        pl.semaphore_signal(barrier, inc=1, device_id=(f + inner, t), device_id_type=MESH)

    ends = (o == 0).astype(jnp.int32) + (o == line_size - 1).astype(jnp.int32)
    pl.semaphore_wait(barrier, G + 1 - ends)

    def place(buf, origin, m, count):
        return buf.at[pl.ds(pl.multiple_of((origin * G + m) * rows, rows), count * rows), :]

    def cut(src, m):
        cols = src.shape[1] // G
        head = (m % slices) * inner + lax.div(m, slices)
        return src.at[:, pl.ds(pl.multiple_of(head * cols, HEAD), cols)]

    def lanes(buf, m, at, cols):
        return place(buf, o, m, 1).at[:, pl.ds(at, cols)]

    def trade(part, buf, ss, rs, d):
        k, src, at = part
        to = (me + d) % G
        dst = lanes(buf, me, at, src.shape[1] // G)
        return remote(cut(src, to), dst, ss.at[k, d], rs.at[k, d], member(to))

    def trade_own(part, buf, sem):
        k, src, at = part
        dst = lanes(buf, me, at, src.shape[1] // G)
        return pltpu.make_async_copy(cut(src, me), dst, sem.at[k])

    def trade_start(parts, buf, ss, rs, sem):
        for part in parts:
            trade_own(part, buf, sem).start()
        for d in range(1, G):
            for part in parts:
                trade(part, buf, ss, rs, d).start()

    def trade_wait(parts, buf, ss, rs, sem, d):
        m = (me + G - d) % G
        for k, src, at in parts:
            if d == 0:
                trade_own((k, src, at), buf, sem).wait()
            else:
                here = lanes(buf, m, at, src.shape[1] // G)
                remote(here, here, ss.at[k, d], rs.at[k, d], member(m)).wait_recv()

    inputs = ((0, query_in, 0), (1, key_in, QC), (2, value_in, QC + HEAD))
    outs = ((0, out_in, 0),)

    def hop(buf, ss, rs, origin, c, way):
        here = place(buf, origin, (me + G - c) % G, 1)
        way_f = f + inner if way == 0 else f - inner
        return remote(here, here, ss.at[way, origin, c], rs.at[origin, c], (way_f, t))

    def forward(buf, ss, rs, s, c):
        below, above = o - s, o + s
        if not isinstance(s, int) or s > 0:
            @pl.when(below >= 0)
            def _():
                hop(buf, ss, rs, below, c, 0).wait_recv()

            @pl.when(above < line_size)
            def _():
                hop(buf, ss, rs, above, c, 0).wait_recv()

        @pl.when(jnp.logical_and(below >= 0, o < line_size - 1))
        def _():
            hop(buf, ss, rs, below, c, 0).start()

        @pl.when(jnp.logical_and(above < line_size, o > 0))
        def _():
            hop(buf, ss, rs, above, c, 1).start()

    def hops_sent(buf, ss, rs, s):
        below, above = o - s, o + s
        for c in range(G):
            hop_sent(buf, ss, rs, below, above, c)

    def hop_sent(buf, ss, rs, below, above, c):
        @pl.when(jnp.logical_and(below >= 0, o < line_size - 1))
        def _():
            hop(buf, ss, rs, below, c, 0).wait_send()

        @pl.when(jnp.logical_and(above < line_size, o > 0))
        def _():
            hop(buf, ss, rs, above, c, 1).wait_send()

    def piece(buf, m, n):
        return buf.at[m, pl.ds(pl.multiple_of(n * span_size, span_size), span_size), :]

    def mine(src, n):
        return src.at[pl.ds(pl.multiple_of(n * span_size, span_size), span_size), :]

    def send_own(src, buf, ss, rs, sem, n):
        for kind, to in ((0, mx), (1, my), (2, mc)):
            remote(
                mine(src, n), piece(buf, me, n), ss.at[kind, n], rs.at[kind, n], member(to)
            ).start()
        pltpu.make_async_copy(mine(src, n), piece(buf, me, n), sem.at[n]).start()

    def arrived(buf, ss, rs, kind, slot, n):
        here = piece(buf, slot, n)
        remote(here, here, ss.at[kind, n], rs.at[kind, n], member(mx)).wait_recv()

    def pass_on(buf, ss, rs, kind, slot, to, n):
        here = piece(buf, slot, n)
        remote(here, here, ss.at[kind, n], rs.at[kind, n], member(to)).start()

    def relay(buf, ss, rs, n, total):
        arrived(buf, ss, rs, 0, mx, n)
        arrived(buf, ss, rs, 1, my, n)

        @pl.when(n < total // 2)
        def _():
            pass_on(buf, ss, rs, 3, mx, my, n)

        @pl.when(n >= total // 2)
        def _():
            pass_on(buf, ss, rs, 3, my, mx, n)

        pass_on(buf, ss, rs, 4, mx, mc, n)
        pass_on(buf, ss, rs, 5, my, mc, n)

    def relay_far(buf, ss, rs, n):
        arrived(buf, ss, rs, 3, md, n)
        pass_on(buf, ss, rs, 6, md, mc, n)

    def settle(src, buf, ss, rs, sem, n):
        pltpu.make_async_copy(mine(src, n), piece(buf, me, n), sem.at[n]).wait()
        for kind, slot in ((2, mc), (4, flip(mx, 2)), (5, flip(my, 2)), (6, flip(md, 2))):
            arrived(buf, ss, rs, kind, slot, n)

    def sent(buf, ss, rs, n):
        for kind in range(7):
            here = piece(buf, me, n)
            remote(here, here, ss.at[kind, n], rs.at[kind, n], member(mx)).wait_send()

    trade_start(inputs, wq, a_send, a_recv, a_own)
    for c in range(G):
        trade_wait(inputs, wq, a_send, a_recv, a_own, c)
        forward(wq, zq_send, zq_recv, 0, c)
        if c == 0:
            for n in range(spans):
                send_own(normed, tokens, t_send, t_recv, t_own, n)
    for c in range(G):
        forward(wq, zq_send, zq_recv, 1, c)
    for n in range(spans):
        relay(tokens, t_send, t_recv, n, spans)
    trade_start(outs, wo, b_send, b_recv, b_own)
    for s in range(2, line_size - 1):
        for c in range(G):
            forward(wq, zq_send, zq_recv, s, c)
    for n in range(spans):
        relay_far(tokens, t_send, t_recv, n)
    for m in range(G):
        trade_wait(outs, wo, b_send, b_recv, b_own, m)
    for c in range(G):
        hop_sent(wq, zq_send, zq_recv, o - (line_size - 2), o + (line_size - 2), c)
        forward(wo, zo_send, zo_recv, 0, c)
    for n in range(spans):
        settle(normed, tokens, t_send, t_recv, t_own, n)
    for c in range(G):
        forward(wq, zq_send, zq_recv, line_size - 1, c)

    pieces = inner * spans
    features = tokens.shape[2]
    scale = HEAD ** (-0.5)

    def chunk_copy(stage, target, ss, rs, p):
        src = stage.at[pl.ds(pl.multiple_of(p * spans * span_size, span_size), spans * span_size), :]
        dst = target.at[:, pl.ds(pl.multiple_of(i * HEAD, HEAD), HEAD)]
        return (
            pltpu.make_async_copy(src, dst, ss.at[p]),
            remote(src, dst, ss.at[p], rs.at[i], (o * inner + p, t)),
        )

    def chunk_arrived(stage, target, ss, rs, p):
        src = stage.at[pl.ds(0, spans * span_size), :]
        dst = target.at[:, pl.ds(pl.multiple_of(p * HEAD, HEAD), HEAD)]
        remote(src, dst, ss.at[p], rs.at[p], (o * inner + p, t)).wait_recv()

    def one_span(n, carry):
        p = lax.div(n, spans)
        part = n % spans
        here = pl.ds(pl.multiple_of(n * span_size, span_size), span_size)
        projected = bias[...]
        for half in range(slices):
            projected = projected + jnp.dot(
                tokens[p * slices + half, pl.ds(pl.multiple_of(part * span_size, span_size), span_size), :],
                wq[pl.ds(half * features, features), :],
                preferred_element_type=jnp.float32,
            )
        cos, sin = cosine[here, :], sine[here, :]

        def turn(x):
            return x * cos + pltpu.roll(x, HEAD // 2, 1) * sin

        size = length[n]
        live = lax.broadcasted_iota(jnp.int32, (span_size, HEAD), 0) < size
        key = jnp.where(live, turn(projected[:, QC : QC + HEAD]), 0.0).astype(jnp.bfloat16)
        value = jnp.where(live, projected[:, QC + HEAD :], 0.0).astype(jnp.bfloat16)
        keys[here, :] = key
        values[here, :] = value
        row = lax.broadcasted_iota(jnp.int32, (span_size, span_size), 0)
        column = lax.broadcasted_iota(jnp.int32, (span_size, span_size), 1)
        allowed = jnp.logical_and(column <= row, column < size)
        for g in range(GROUPS):
            query = turn(projected[:, g * HEAD : (g + 1) * HEAD]).astype(jnp.bfloat16)
            scores = lax.dot_general(
                query, key, (((1,), (1,)), ((), ())), preferred_element_type=jnp.float32
            ) * scale
            scores = jnp.where(allowed, scores, -1e30)
            raised = jnp.exp(scores - jnp.max(scores, axis=-1, keepdims=True))
            probs = (raised / jnp.sum(raised, axis=-1, keepdims=True)).astype(jnp.bfloat16)
            own[here, g * HEAD : (g + 1) * HEAD] = jnp.dot(
                probs, value, preferred_element_type=jnp.float32
            ).astype(jnp.bfloat16)
        send_own(own, gathered, g_send, g_recv, g_own, n)
        for half in range(2):
            turn_c = (2 * n + half) % G
            forward(wo, zo_send, zo_recv, 1 + lax.div(2 * n, G), turn_c)

        @pl.when(n >= 1)
        def _():
            relay(gathered, g_send, g_recv, n - 1, pieces)

        @pl.when(n >= 2)
        def _():
            relay_far(gathered, g_send, g_recv, n - 2)

        return carry

    lax.fori_loop(0, pieces, one_span, 0)
    for p in range(inner):
        for stage, target, ss, rs in (
            (keys, key_out, k_send, k_recv),
            (values, value_out, v_send, v_recv),
        ):
            near, far = chunk_copy(stage, target, ss, rs, p)
            pl.when(i == p)(near.start)
            pl.when(i != p)(far.start)
    relay(gathered, g_send, g_recv, pieces - 1, pieces)
    relay_far(gathered, g_send, g_recv, pieces - 2)
    relay_far(gathered, g_send, g_recv, pieces - 1)

    def fetch(n):
        return pltpu.make_async_copy(
            gathered.at[:, pl.ds(pl.multiple_of(n * span_size, span_size), span_size), :],
            buffer.at[n % 2],
            load.at[n % 2],
        )

    def deliver(n):
        p, part = lax.div(n, spans), n % spans
        src = mine(result, n)
        dst = out.at[
            pl.ds(pl.multiple_of(part * span_size, span_size), span_size),
            pl.ds(pl.multiple_of(i * QC, HEAD), QC),
        ]
        return (
            p,
            pltpu.make_async_copy(src, dst, r_send.at[n]),
            remote(src, dst, r_send.at[n], r_recv.at[i, part], (o * inner + p, t)),
        )

    settle(own, gathered, g_send, g_recv, g_own, 0)
    fetch(0).start()
    for n in range(spans):
        sent(tokens, t_send, t_recv, n)

    far = jnp.where(o < line_size // 2, line_size - 1, 0)
    per = G // line_size

    def head_of(slab, e):
        head = slab * per + e
        return (
            (head % inner) * slices + lax.div(head, inner),
            wo[pl.ds(pl.multiple_of(head * QC, QC), QC), :],
        )

    def near_tile(n, carry):
        @pl.when(n + 1 < pieces)
        def _():
            settle(own, gathered, g_send, g_recv, g_own, n + 1)
            fetch(n + 1).start()

        fetch(n).wait()
        total = jnp.zeros((span_size, QC), jnp.float32)
        for j in range(1, line_size):
            for e in range(per):
                m, weight = head_of((far + j) % line_size, e)
                total = total + jnp.dot(
                    buffer[n % 2, m], weight, preferred_element_type=jnp.float32
                )
        partial[n] = total
        for e in range(per):
            m, _ = head_of(far, e)
            tokens[n, e * span_size : (e + 1) * span_size, :QC] = buffer[n % 2, m]
        return carry

    lax.fori_loop(0, pieces, near_tile, 0)
    for s in range(1 + 2 * pieces // G, line_size):
        for c in range(G):
            forward(wo, zo_send, zo_recv, s, c)

    def far_tile(n, carry):
        total = partial[n]
        for e in range(per):
            _, weight = head_of(far, e)
            total = total + jnp.dot(
                tokens[n, e * span_size : (e + 1) * span_size, :QC],
                weight,
                preferred_element_type=jnp.float32,
            )
        result[pl.ds(pl.multiple_of(n * span_size, span_size), span_size), :] = total.astype(
            jnp.bfloat16
        )
        p, near, away = deliver(n)
        pl.when(i == p)(near.start)
        pl.when(i != p)(away.start)
        return carry

    lax.fori_loop(0, pieces, far_tile, 0)

    for s in range(line_size):
        if s != line_size - 2:
            hops_sent(wq, zq_send, zq_recv, s)
        hops_sent(wo, zo_send, zo_recv, s)
    for d in range(1, G):
        for part in inputs:
            trade(part, wq, a_send, a_recv, d).wait_send()
        for part in outs:
            trade(part, wo, b_send, b_recv, d).wait_send()

    def last(n, carry):
        sent(gathered, g_send, g_recv, n)
        p, near, far = deliver(n)
        pl.when(i == p)(near.wait)
        pl.when(i != p)(far.wait_send)
        return carry

    lax.fori_loop(0, pieces, last, 0)
    for p in range(inner):
        for stage, target, ss, rs in (
            (keys, key_out, k_send, k_recv),
            (values, value_out, v_send, v_recv),
        ):
            near, far = chunk_copy(stage, target, ss, rs, p)
            pl.when(i == p)(near.wait)

            @pl.when(i != p)
            def _():
                far.wait_send()
                chunk_arrived(stage, target, ss, rs, p)

        @pl.when(i != p)
        def _():
            for part in range(spans):
                dst = out.at[pl.ds(part * span_size, span_size), pl.ds(p * QC, QC)]
                remote(
                    mine(result, 0), dst, r_send.at[0], r_recv.at[p, part], (o * inner + p, t)
                ).wait_recv()


def fused(members, slices, spans, span_size, normed, weights, bias, cosine, sine, length):
    inner = G // slices
    line_size = members // inner
    token_rows, features = normed.shape
    rows = weights[0].shape[0]
    depth = members * slices * rows
    every = inner * token_rows
    pieces = inner * spans
    bf16 = jnp.bfloat16
    dma = pltpu.SemaphoreType.DMA
    hops = [dma((2, line_size, G)), dma((line_size, G))]
    anywhere = pl.BlockSpec(memory_space=pl.ANY)
    vmem = pl.BlockSpec(memory_space=pltpu.VMEM)
    return pl.pallas_call(
        functools.partial(body, members, slices, spans, span_size),
        out_shape=[
            jax.ShapeDtypeStruct((token_rows, inner * QC), bf16),
            jax.ShapeDtypeStruct((token_rows, inner * HEAD), bf16),
            jax.ShapeDtypeStruct((token_rows, inner * HEAD), bf16),
            jax.ShapeDtypeStruct((G, every, QC), bf16),
        ],
        in_specs=[anywhere] * 5 + [vmem] * 3 + [pl.BlockSpec(memory_space=pltpu.SMEM)],
        out_specs=[anywhere] * 4,
        scratch_shapes=[
            pltpu.VMEM((depth, QC + 2 * HEAD), bf16),
            pltpu.VMEM((depth, QC), bf16),
            pltpu.VMEM((G, token_rows, features), bf16),
            pltpu.VMEM((every, QC), bf16),
            pltpu.VMEM((every, HEAD), bf16),
            pltpu.VMEM((every, HEAD), bf16),
            pltpu.VMEM((every, QC), bf16),
            pltpu.VMEM((2, G, span_size, QC), bf16),
            pltpu.VMEM((pieces, span_size, QC), jnp.float32),
            dma((3, G)), dma((3, G)), dma((3,)),
            dma((1, G)), dma((1, G)), dma((1,)),
            *hops, *hops,
            dma((7, spans)), dma((7, spans)), dma((spans,)),
            dma((7, pieces)), dma((7, pieces)), dma((pieces,)),
            dma((2,)),
            dma((pieces,)), dma((inner, spans)),
            dma((inner,)), dma((inner,)),
            dma((inner,)), dma((inner,)),
        ],
        compiler_params=pltpu.CompilerParams(
            collective_id=0, has_side_effects=True, vmem_limit_bytes=61 * 1024 * 1024
        ),
    )(normed, *weights, bias, cosine, sine, length)


def local(
    hidden_in,
    norm_gain,
    query_weight,
    key_weight,
    value_weight,
    out_weight,
    query_bias,
    key_bias,
    value_bias,
    span_start,
    span_length,
):
    slices = lax.axis_size("tensor")
    members = lax.axis_size("fsdp")
    devices = slices * members
    inner = KV_HEADS // slices
    outer = devices // KV_HEADS
    line = lax.axis_index("fsdp") // inner
    i = lax.axis_index("fsdp") % inner
    t = lax.axis_index("tensor")
    token_rows, features = hidden_in.shape
    local_spans = span_start.shape[0]
    span_size = token_rows // local_spans
    learner_rows = query_weight.shape[0]
    qc = GROUPS * HEAD
    oc = out_weight.shape[1] // KV_HEADS

    def xor(x, k):
        return lax.ppermute(x, AXES, [(d, d ^ k) for d in range(devices)])

    def shift(x, step):
        pairs = [
            (d, d + step * KV_HEADS)
            for d in range(devices)
            if 0 <= d + step * KV_HEADS < devices
        ]
        return lax.ppermute(x, AXES, pairs)

    def gather_group(own):
        half = own.shape[0] // 2
        one = xor(own, 1)
        four = xor(own, 4)
        five = jnp.concatenate([xor(four[:half], 1), xor(one[half:], 4)], axis=0)
        got = {0: own, 1: one, 4: four, 5: five}
        for k in (0, 1, 4, 5):
            got[k ^ 2] = xor(got[k], 2)
        return [got[k] for k in range(KV_HEADS)]

    def blocks(weight):
        cols = weight.shape[1] // KV_HEADS
        cut = weight.reshape(learner_rows, slices, inner, cols)
        return jnp.transpose(cut, (2, 1, 0, 3)).reshape(KV_HEADS, learner_rows, cols)

    def exchange(stacked):
        groups = [[g * KV_HEADS + j for j in range(KV_HEADS)] for g in range(outer)]
        arrived = lax.all_to_all(
            stacked, AXES, split_axis=0, concat_axis=0, axis_index_groups=groups, tiled=True
        )
        return arrived.reshape(KV_HEADS * learner_rows, stacked.shape[2])

    def gather_line(slab):
        below, above = [], []
        up = down = slab
        for _ in range(outer - 1):
            up = shift(up, 1)
            down = shift(down, -1)
            below.append(up)
            above.append(down)
        every = jnp.stack(below[::-1] + [slab] + above)
        whole = lax.dynamic_slice_in_dim(every, outer - 1 - line, outer, axis=0)
        return whole.reshape(outer * slab.shape[0], slab.shape[1])

    def unswap(parts):
        parts = list(parts)
        bit = 1
        while bit < inner:
            flip = (i & bit) != 0
            parts = [jnp.where(flip, parts[p ^ bit], parts[p]) for p in range(inner)]
            bit *= 2
        return parts

    joined = jnp.concatenate(
        [blocks(query_weight), blocks(key_weight), blocks(value_weight)], axis=2
    )
    out_blocks = blocks(out_weight)
    source = hidden_in.astype(jnp.float32)
    squares = jnp.sum(source * source, axis=-1, keepdims=True)
    bit = 1
    while bit < slices:
        squares = squares + xor(squares, bit)
        bit *= 2
    inverse_rms = lax.rsqrt(squares / (features * slices) + epsilon)
    gain = lax.dynamic_slice_in_dim(norm_gain, t * features, features).astype(jnp.float32)
    normed = (source * inverse_rms * gain).astype(jnp.bfloat16)
    bias = jnp.concatenate(
        [
            lax.dynamic_slice_in_dim(query_bias, i * qc, qc),
            lax.dynamic_slice_in_dim(key_bias, i * HEAD, HEAD),
            lax.dynamic_slice_in_dim(value_bias, i * HEAD, HEAD),
        ]
    ).astype(jnp.float32)
    marks = jnp.stack([span_start, span_length])
    marks = [marks] + [xor(marks, ki * slices) for ki in range(1, inner)]
    if (
        learner_rows % 16 == 0
        and outer in (4, 8)
        and inner * local_spans == KV_HEADS
        and local_spans >= KV_HEADS // outer
        and features >= qc
    ):
        marks = jnp.concatenate(unswap(marks), axis=1)
        cosine, sine = angles(marks[0], span_size)
        cosine, sine = cosine[:, 0], sine[:, 0]
        return tuple(
            fused(
                members, slices, local_spans, span_size, normed,
                (query_weight, key_weight, value_weight, out_weight),
                bias[None, :],
                jnp.concatenate([cosine, cosine], axis=1),
                jnp.concatenate([-sine, sine], axis=1),
                marks[1],
            )[:3]
        )

    tokens = gather_group(normed)
    weight = gather_line(exchange(joined))
    out_whole = gather_line(exchange(out_blocks))
    rows = jnp.arange(span_size, dtype=jnp.int32)[:, None]
    columns = jnp.arange(span_size, dtype=jnp.int32)[None, :]
    halves = [
        lax.dynamic_slice_in_dim(weight, (t ^ kt) * features, features) for kt in range(slices)
    ]
    mixes, key_parts, value_parts = [], [], []
    for ki in range(inner):
        projected = bias[None, :]
        for kt in range(slices):
            projected = projected + jnp.dot(
                tokens[ki * slices + kt], halves[kt], preferred_element_type=jnp.float32
            )
        start, length = marks[ki][0], marks[ki][1]
        cosine, sine = angles(start, span_size)
        query = rotate(
            projected[:, :qc].reshape(token_rows, GROUPS, HEAD), cosine, sine
        ).astype(jnp.bfloat16)
        keys = rotate(projected[:, None, qc : qc + HEAD], cosine, sine)[:, 0]
        live = (columns < length[:, None]).reshape(token_rows, 1)
        key_cache = jnp.where(live, keys, 0.0).astype(jnp.bfloat16)
        value_cache = jnp.where(live, projected[:, qc + HEAD :], 0.0).astype(jnp.bfloat16)
        query_blocks = query.reshape(local_spans, span_size, GROUPS, HEAD)
        key_blocks = key_cache.reshape(local_spans, span_size, HEAD)
        value_blocks = value_cache.reshape(local_spans, span_size, HEAD)
        scores = jnp.einsum(
            "sqgd,std->sgqt", query_blocks, key_blocks, preferred_element_type=jnp.float32
        ) * HEAD ** (-0.5)
        allowed = (columns <= rows)[None] & (columns[None] < length[:, None, None])
        scores = jnp.where(allowed[:, None], scores, -1e30)
        highest = jnp.max(scores, axis=-1, keepdims=True)
        raised = jnp.exp(scores - highest)
        probs = (raised / jnp.sum(raised, axis=-1, keepdims=True)).astype(jnp.bfloat16)
        mixed = jnp.einsum(
            "sgqt,std->sqgd", probs, value_blocks, preferred_element_type=jnp.float32
        )
        mixes.append(mixed.reshape(token_rows, qc).astype(jnp.bfloat16))
        key_parts.append(key_cache if ki == 0 else xor(key_cache, ki * slices))
        value_parts.append(value_cache if ki == 0 else xor(value_cache, ki * slices))

    mixes = unswap(mixes)
    attended = gather_group(jnp.concatenate(mixes, axis=0))
    combined = 0.0
    for k in range(KV_HEADS):
        head = (t ^ (k % slices)) * inner + (i ^ (k // slices))
        combined = combined + jnp.dot(
            attended[k],
            lax.dynamic_slice_in_dim(out_whole, head * qc, qc),
            preferred_element_type=jnp.float32,
        )
    result = combined.astype(jnp.bfloat16).reshape(inner, token_rows, oc)
    result = unswap([result[p] for p in range(inner)])
    out_parts = [result[0]] + [xor(result[ki], ki * slices) for ki in range(1, inner)]
    return tuple(
        jnp.concatenate(unswap(parts), axis=1)
        for parts in (out_parts, key_parts, value_parts)
    )


def solution(mesh):
    placed = (
        P("fsdp", "tensor"),
        P(),
        P(("fsdp", "tensor"), None),
        P(("fsdp", "tensor"), None),
        P(("fsdp", "tensor"), None),
        P(("fsdp", "tensor"), None),
        P("tensor"),
        P("tensor"),
        P("tensor"),
        P("fsdp"),
        P("fsdp"),
    )
    return jax.shard_map(
        local,
        mesh=mesh,
        in_specs=placed,
        out_specs=(P("fsdp", "tensor"), P("fsdp", "tensor"), P("fsdp", "tensor")),
        check_vma=False,
    )
```
